32 devices in a mesh: ty: 8 (over z, x), tx: 4 (over y, core).
Axes of the slice: x: 2, y: 2, z: 4, core: 2. Of those that a mesh axis runs over, the one named last changes fastest.
Arguments:
- fixed_image: float32 [512, 1024], P('ty', 'tx'), may hold values from -6 to 6
- moving_image: float32 [512, 1024], P('ty', 'tx'), may hold values from -6 to 6
- tissue: int32 [16, 32], P('ty', 'tx'), may hold values from 0 to 1, as said below
Outputs:
- coefficients: float32 [2, 16, 32], P(None, 'ty', 'tx')
- mismatch: float32 [512, 1024], P('ty', 'tx')
The draws below stay inside these ranges and needn't reach their ends.
Inputs may be any that keep to these rules, and one draw needn't show every extreme that they name: 1 marks a block of 32 x 32 fine pixels that holds tissue, 0 background.
All inputs are finite; a program needn't handle non-finite values.
Results may differ from the reference program's by a relative error of at most 0.0003.
Values sent between devices are 32-bit elements; how exact they have to be, the bound alone decides.
A program may use at most 64 MiB of HBM per device.

```python
import jax
import jax.numpy as jnp
from jax import lax

SPACE = 32
HALO = 6
MB = 32
ITERS = 2
H = 512
W = 1024
CR = 16
CC = 32
NBY = 16
NBX = 32


def draw_tissue(key, part):
    subkeys = jax.random.split(key, 5)
    row_index = lax.broadcasted_iota(jnp.int32, (NBY, NBX), 0)
    col_index = lax.broadcasted_iota(jnp.int32, (NBY, NBX), 1)
    centre_y = jax.random.randint(subkeys[0], (4,), 0, NBY)
    centre_x = jax.random.randint(subkeys[1], (4,), 0, NBX)
    radius_y = jax.random.randint(subkeys[2], (4,), max(NBY // 8, 1), max(NBY // 3, 2) + 1)
    radius_x = jax.random.randint(subkeys[3], (4,), max(NBX // 8, 1), max(NBX // 3, 2) + 1)
    inside = row_index < 0
    for centre_index in range(4):
        gap_y = row_index - centre_y[centre_index]
        gap_x = col_index - centre_x[centre_index]
        reach_y = radius_y[centre_index] * radius_y[centre_index]
        reach_x = radius_x[centre_index] * radius_x[centre_index]
        inside = inside | (gap_y * gap_y * reach_x + gap_x * gap_x * reach_y <= reach_y * reach_x)
    hole_mask = jax.random.randint(subkeys[4], (NBY, NBX), 0, 12) == 0
    return jnp.where(inside & jnp.logical_not(hole_mask), 1, 0).astype(jnp.int32)


def steps_of(own_key, shape, shards, smallest, largest):
    factor_of = 1.0
    for dim, shards_of in shards:
        heights = jax.random.uniform(jax.random.fold_in(jax.random.fold_in(own_key, 6), dim), (shards_of,), jnp.float32, smallest / len(shards), largest / len(shards))
        factor_of = factor_of * jnp.repeat(jnp.exp(heights), shape[dim] // shards_of).reshape((-1,) + (1,) * (len(shape) - 1 - dim))
    return factor_of


def scatter_about(stream_key, dims, width, reach, cuts=(), held_as=jnp.bfloat16):
    gain = steps_of(stream_key, dims, cuts, -0.22, 0.18) if cuts else 1.0
    array = jax.random.normal(stream_key, dims, jnp.float32) * width * gain
    return jnp.minimum(jnp.maximum(array, -reach), reach).astype(held_as)


def setup_inputs(seed: int = 0) -> dict:
    arg_keys = jax.random.split(jax.random.key(seed), 4)
    return {
        "fixed_image": scatter_about(arg_keys[0], (H, W), 1.0, 6.0, ((0, 8), (1, 4)), jnp.float32),
        "moving_image": scatter_about(arg_keys[1], (H, W), 1.0, 6.0, ((0, 8), (1, 4)), jnp.float32),
        "tissue": draw_tissue(jax.random.fold_in(arg_keys[3], 71), 0),
    }


offset_pairs = ((0, 2), (0, -2), (2, 0), (-2, 0), (2, 2), (2, -2), (-2, 2), (-2, -2), (0, 4), (0, -4), (4, 0), (-4, 0))
highest = lax.Precision.HIGHEST


def bspline(values):
    magnitude = jnp.abs(values)
    near_part = 2.0 / 3.0 - magnitude * magnitude + 0.5 * magnitude ** 3
    far_part = (2.0 - magnitude) ** 3 / 6.0
    return jnp.where(magnitude < 1.0, near_part, jnp.where(magnitude < 2.0, far_part, 0.0 * magnitude))


def box_mean(values):
    height, breadth = values.shape
    total = values[0:height - 2, 0:breadth - 2]
    for shift_y in range(3):
        for shift_x in range(3):
            if shift_y + shift_x > 0:
                total = total + values[shift_y:height - 2 + shift_y, shift_x:breadth - 2 + shift_x]
    return total / 9.0


def descriptors(padded):
    height, breadth = padded.shape
    centre = padded[4:height - 4, 4:breadth - 4]
    distances = []
    for offset_y, offset_x in offset_pairs:
        shifted = padded[4 + offset_y:height - 4 + offset_y, 4 + offset_x:breadth - 4 + offset_x]
        distances.append(box_mean((centre - shifted) ** 2))
    variance = sum(distances) / 12.0 + 0.1
    return [jnp.exp(-member / variance) for member in distances]


def level_terms(fixed_padded, moving_padded, factor):
    fixed_mind = descriptors(fixed_padded)
    moving_mind = descriptors(moving_padded)
    summed = None
    for fixed_part, moving_part in zip(fixed_mind, moving_mind):
        differ = moving_part[1:-1, 1:-1] - fixed_part[1:-1, 1:-1]
        slope_y = (moving_part[2:, 1:-1] - moving_part[:-2, 1:-1]) / (2.0 * factor)
        slope_x = (moving_part[1:-1, 2:] - moving_part[1:-1, :-2]) / (2.0 * factor)
        parts = (differ * slope_y, differ * slope_x, slope_y * slope_y, slope_y * slope_x, slope_x * slope_x, differ * differ)
        summed = parts if summed is None else tuple(left + right for left, right in zip(summed, parts))
    return summed


def spline_matrix(length, factor, cell_count):
    position = factor * jnp.arange(length, dtype=jnp.float32) + (factor - 1) / 2.0
    knots = jnp.arange(cell_count, dtype=jnp.float32)
    return bspline(position[:, None] / SPACE - knots[None, :])


def expand_mask(tissue, factor):
    side = MB // factor
    block_rows, block_cols = tissue.shape
    spread = jnp.broadcast_to(tissue.astype(jnp.float32)[:, None, :, None], (block_rows, side, block_cols, side))
    return spread.reshape(block_rows * side, block_cols * side)


def displace(left, control, right):
    return jnp.stack([jnp.dot(jnp.dot(left, control[member], precision=highest), right.T, precision=highest) for member in range(2)])


def pool_image(image):
    height, breadth = image.shape
    return image.reshape(height // 2, 2, breadth // 2, 2).mean(axis=(1, 3))


def gradient_terms(summed, weight, field):
    return jnp.stack([weight * (summed[0] + summed[2] * field[0] + summed[3] * field[1]),
                      weight * (summed[1] + summed[3] * field[0] + summed[4] * field[1])])


def curvature_density(summed, weight, motion):
    return weight * (motion[0] * (summed[2] * motion[0] + summed[3] * motion[1])
                     + motion[1] * (summed[3] * motion[0] + summed[4] * motion[1]))


def mismatch_of(summed, field):
    return (summed[5] + 2.0 * (summed[0] * field[0] + summed[1] * field[1])
            + field[0] * (summed[2] * field[0] + summed[3] * field[1])
            + field[1] * (summed[3] * field[0] + summed[4] * field[1]))


def reference(fixed_image, moving_image, tissue):
    coefficients = jnp.zeros((2, CR, CC), jnp.float32)
    summed = None
    field = None
    for factor in (2, 1):
        if factor == 2:
            fixed_level = pool_image(fixed_image)
            moving_level = pool_image(moving_image)
        else:
            fixed_level = fixed_image
            moving_level = moving_image
        summed = level_terms(jnp.pad(fixed_level, HALO), jnp.pad(moving_level, HALO), factor)
        rows_matrix = spline_matrix(fixed_level.shape[0], factor, CR)
        cols_matrix = spline_matrix(fixed_level.shape[1], factor, CC)
        weight = expand_mask(tissue, factor)
        field = displace(rows_matrix, coefficients, cols_matrix)
        for iteration in range(ITERS):
            pixel_grad = gradient_terms(summed, weight, field)
            direction = jnp.stack([jnp.dot(jnp.dot(rows_matrix.T, pixel_grad[member], precision=highest), cols_matrix, precision=highest) for member in range(2)])
            motion = displace(rows_matrix, direction, cols_matrix)
            norm_sum = jnp.sum(direction * direction)
            curvature = jnp.sum(curvature_density(summed, weight, motion))
            step_size = norm_sum / curvature
            coefficients = coefficients - step_size * direction
            field = field - step_size * motion
    return coefficients, mismatch_of(summed, field)
```

```python
import functools

import jax
import jax.numpy as jnp
from jax import lax
from jax.experimental import pallas as pl
from jax.experimental.pallas import tpu as pltpu
from jax.sharding import PartitionSpec as P

SPACE = 32
REACH_Y = 5
REACH_X = 11
RIM = 16
MESH = pl.DeviceIdType.MESH
F32 = jnp.float32

half_offsets = ((0, 2), (2, 0), (2, 2), (2, -2), (0, 4), (4, 0))
travels = ((-1, 0), (1, 0), (0, -1), (0, 1), (-1, -1), (-1, 1), (1, -1), (1, 1))


def bspline(values):
    magnitude = jnp.abs(values)
    near_part = 2.0 / 3.0 - magnitude * magnitude + 0.5 * magnitude * magnitude * magnitude
    rest = 2.0 - magnitude
    far_part = rest * rest * rest / 6.0
    return jnp.where(magnitude < 1.0, near_part, jnp.where(magnitude < 2.0, far_part, 0.0))


def moved(values, by_y, by_x):
    rows, lanes = values.shape
    if by_x:
        values = pltpu.roll(values, (-by_x) % lanes, 1)
    if by_y:
        values = pltpu.roll(values, (-by_y) % rows, 0)
    return values


def minds_into(image, lane_step, out_ref):
    total = None
    for index, (offset_y, offset_x) in enumerate(half_offsets):
        gap = image - moved(image, offset_y, lane_step * offset_x)
        square = gap * gap
        rows = square + moved(square, 1, 0) + moved(square, -1, 0)
        box = rows + moved(rows, 0, lane_step) + moved(rows, 0, -lane_step)
        other = moved(box, -offset_y, -lane_step * offset_x)
        out_ref[2 * index, : image.shape[0]] = box
        out_ref[2 * index + 1, : image.shape[0]] = other
        both = box + other
        total = both if total is None else total + both
    return -1.0 / (total / 12.0 + 0.9)


def terms_into(fixed, moving, lane_step, factor, fixed_ref, moving_ref, terms_ref, wide):
    rows = fixed.shape[0]
    height = rows - 16
    fixed_scale = minds_into(fixed, lane_step, fixed_ref)[8 : 8 + height, :wide]
    moving_scale = minds_into(moving, lane_step, moving_ref)
    sums = None
    for index in range(12):
        fixed_mind = jnp.exp(fixed_ref[index, 8 : 8 + height, :wide] * fixed_scale)
        mind = jnp.exp(moving_ref[index, :rows] * moving_scale)
        differ = mind[8 : 8 + height, :wide] - fixed_mind
        slope_y = moved(mind[:, :wide], 1, 0) - moved(mind[:, :wide], -1, 0)
        slope_y = slope_y[8 : 8 + height]
        own = mind[8 : 8 + height]
        slope_x = (moved(own, 0, lane_step) - moved(own, 0, -lane_step))[:, :wide]
        parts = (
            differ * slope_y,
            differ * slope_x,
            slope_y * slope_y,
            slope_y * slope_x,
            slope_x * slope_x,
            differ * differ,
        )
        sums = parts if sums is None else tuple(a + b for a, b in zip(sums, parts))
    once = 1.0 / (2.0 * factor)
    scales = (once, once, once * once, once * once, once * once, 1.0)
    for index in range(6):
        terms_ref[index] = sums[index] * scales[index]


def kernel(
    count_y,
    count_x,
    widths,
    tissue_ref,
    fixed_ref,
    moving_ref,
    coef_ref,
    mismatch_ref,
    mid,
    left_side,
    right_side,
    full,
    fixed_minds,
    moving_minds,
    fine_terms,
    coarse_terms,
    fine_weight,
    coarse_weight,
    fine_rows,
    coarse_rows,
    fine_cols,
    coarse_cols,
    grid_sum,
    *rest,
):
    rounds = len(widths)
    boxes = rest[:rounds]
    rim_send, rim_recv, send_sem, recv_sem = rest[rounds:]
    ty = lax.axis_index("ty")
    tx = lax.axis_index("tx")
    count = count_y * count_x
    me = ty * count_x + tx
    height, breadth = fixed_ref.shape
    knots = count_x * (breadth // SPACE)
    cells_y, cells_x = height // SPACE, breadth // SPACE

    def peer(step):
        other = lax.rem(me + step, count)
        return (other // count_x, lax.rem(other, count_x))

    def for_peers(act):
        if count <= 64:
            for step in range(1, count):
                act(peer(step))
        else:

            def body(step, carry):
                act(peer(step))
                return carry

            lax.fori_loop(1, count, body, 0)

    low, high = slice(0, RIM), slice(RIM + height, 2 * RIM + height)

    @pl.when(ty == 0)
    def _():
        for ref in (mid, left_side, right_side):
            ref[:, low] = jnp.zeros((2, RIM, ref.shape[2]), F32)

    @pl.when(ty == count_y - 1)
    def _():
        for ref in (mid, left_side, right_side):
            ref[:, high] = jnp.zeros((2, RIM, ref.shape[2]), F32)

    @pl.when(tx == 0)
    def _():
        left_side[...] = jnp.zeros(left_side.shape, F32)

    @pl.when(tx == count_x - 1)
    def _():
        right_side[...] = jnp.zeros(right_side.shape, F32)

    barrier = pltpu.get_barrier_semaphore()
    for_peers(
        lambda device: pl.semaphore_signal(barrier, 1, device_id=device, device_id_type=MESH)
    )

    lane = lax.broadcasted_iota(jnp.int32, (8, breadth), 1)
    for k in range(REACH_X):
        fine_cols[k] = bspline(lane.astype(F32) / SPACE - (k - 1.0))
        coarse_cols[k] = bspline((lane.astype(F32) + 0.5) / SPACE - (k - 1.0))
    row = lax.broadcasted_iota(jnp.int32, (height, 128), 0).astype(F32)
    coarse_row = lax.broadcasted_iota(jnp.int32, (height // 2, 128), 0).astype(F32)
    for r in range(REACH_Y):
        fine_rows[r] = bspline(row / SPACE - (r - 1.0))
        coarse_rows[r] = bspline((2.0 * coarse_row + 0.5) / SPACE - (r - 1.0))
    even = lax.rem(lane, 2) == 0
    for i in range(cells_y):
        line = jnp.zeros((8, breadth), F32)
        for j in range(cells_x):
            value = tissue_ref[i, j].astype(F32)
            inside = (lane >= j * SPACE) & (lane < (j + 1) * SPACE)
            line = jnp.where(inside, value, line)
        half = jnp.where(even, line, 0.0)
        for part in range(SPACE // 8):
            start = i * SPACE + part * 8
            fine_weight[start : start + 8] = line
        for part in range(SPACE // 16):
            start = i * (SPACE // 2) + part * 8
            coarse_weight[start : start + 8] = half

    pl.semaphore_wait(barrier, count - 1)

    def rows_of(travel):
        if travel == 0:
            return slice(0, height), slice(RIM, RIM + height)
        if travel > 0:
            return slice(height - RIM, height), low
        return slice(0, RIM), high

    def landing(travel_y, travel_x):
        ref = mid if travel_x == 0 else (left_side if travel_x > 0 else right_side)
        return ref.at[:, rows_of(travel_y)[1]]

    def exists(travel_y, travel_x):
        to_y, to_x = ty + travel_y, tx + travel_x
        return (to_y >= 0) & (to_y < count_y) & (to_x >= 0) & (to_x < count_x)

    for index, (travel_y, travel_x) in enumerate(travels):

        @pl.when(exists(travel_y, travel_x))
        def _():
            source_rows = rows_of(travel_y)[0]
            if travel_x == 0:
                lanes = slice(0, breadth)
            elif travel_x > 0:
                lanes = slice(breadth - 128, breadth)
            else:
                lanes = slice(0, 128)
            for image, ref in enumerate((fixed_ref, moving_ref)):
                pltpu.make_async_remote_copy(
                    src_ref=ref.at[source_rows, lanes],
                    dst_ref=landing(travel_y, travel_x).at[image],
                    send_sem=rim_send.at[index],
                    recv_sem=rim_recv.at[index],
                    device_id=(ty + travel_y, tx + travel_x),
                    device_id_type=MESH,
                ).start()

    for image, ref in enumerate((fixed_ref, moving_ref)):
        mid[image, RIM : RIM + height] = ref[...]

    for index, (travel_y, travel_x) in enumerate(travels):

        @pl.when(exists(-travel_y, -travel_x))
        def _():
            place = landing(travel_y, travel_x)
            pltpu.make_async_copy(place, place, rim_recv.at[index]).wait()

    tiles = breadth // 128
    side_lane = lax.broadcasted_iota(jnp.int32, (height + 2 * RIM, 128), 1)
    for image in range(2):
        for tile in range(tiles):
            full[image * (tiles + 1) + tile] = mid[image, :, tile * 128 : (tile + 1) * 128]
        full[image * (tiles + 1) + tiles] = jnp.where(
            side_lane < 64, right_side[image], left_side[image]
        )

    def fine_image(image):
        base = image * (tiles + 1)
        return jnp.concatenate(
            [full[base + tile, 8 : height + 24] for tile in range(tiles + 1)], axis=1
        )

    def coarse_image(image):
        base = image * (tiles + 1)
        span = height // 2 + RIM
        summed = jnp.concatenate(
            [
                full[base + tile, pl.ds(0, span, stride=2), :]
                + full[base + tile, pl.ds(1, span, stride=2), :]
                for tile in range(tiles + 1)
            ],
            axis=1,
        )
        return 0.25 * (summed + moved(summed, 0, 1))

    terms_into(
        coarse_image(0), coarse_image(1), 2, 2, fixed_minds, moving_minds, coarse_terms, breadth
    )

    small_lane = lax.broadcasted_iota(jnp.int32, (8, 128), 1)
    small_row = lax.broadcasted_iota(jnp.int32, (8, 128), 0)
    first_knot = tx * cells_x - 1
    valid = (
        (small_lane < REACH_X)
        & (small_lane + first_knot >= 0)
        & (small_lane + first_knot < knots)
    )

    def displace(window, rows_ref, cols_ref):
        fields = []
        for member in range(2):
            line = None
            for k in range(REACH_X):
                part = window[member][:, k : k + 1] * cols_ref[k]
                line = part if line is None else line + part
            field = None
            for r in range(REACH_Y):
                weights = jnp.concatenate([rows_ref[r]] * tiles, axis=1)
                part = weights * line[r : r + 1, :]
                field = part if field is None else field + part
            fields.append(field)
        return fields

    def gather_up(pixels, rows_ref, cols_ref):
        compact = []
        for member in range(2):
            lines = []
            for r in range(REACH_Y):
                weights = jnp.concatenate([rows_ref[r]] * tiles, axis=1)
                lines.append(jnp.sum(weights * pixels[member], axis=0, keepdims=True))
            lines.append(jnp.zeros((8 - REACH_Y, breadth), F32))
            line = jnp.concatenate(lines, axis=0)
            out = jnp.zeros((8, 128), F32)
            for k in range(REACH_X):
                column = jnp.sum(line * cols_ref[k], axis=1, keepdims=True)
                out = jnp.where(small_lane == k, column, out)
            compact.append(jnp.where(valid, out, 0.0))
        return compact

    def message(sets, width):
        out = [None] * (width // 128)
        for number, members in enumerate(sets):
            for member in range(2):
                start = (2 * number + member) * knots
                shift = lax.rem(first_knot + 128 + start % 128, 128)
                part = pltpu.roll(members[member], shift, 1)
                at = start // 128
                out[at] = part if out[at] is None else out[at] + part
        return out

    def send(turn, pieces):
        box = boxes[turn]
        for at, piece in enumerate(pieces):
            box[me, :, at * 128 : (at + 1) * 128] = piece

        def act(device):
            pltpu.make_async_remote_copy(
                src_ref=box.at[me],
                dst_ref=box.at[me],
                send_sem=send_sem.at[turn],
                recv_sem=recv_sem.at[turn],
                device_id=device,
                device_id_type=MESH,
            ).start()

        for_peers(act)

    def arrive(turn):
        part = boxes[turn].at[0 : count - 1]
        pltpu.make_async_copy(part, part, recv_sem.at[turn]).wait()

    grid_rows = grid_sum.shape[0]

    def collect(turn, set_count):
        width = widths[turn]
        wide_row = lax.broadcasted_iota(jnp.int32, (8, width), 0)
        grid_sum[:, :width] = jnp.zeros((grid_rows, width), F32)
        extra = None
        for t in range(count_y):
            tile = boxes[turn][t * count_x]
            for j in range(1, count_x):
                tile = tile + boxes[turn][t * count_x + j]
            extra = tile if extra is None else extra + tile
            if set_count:
                grid_sum[2 * t : 2 * t + 8, :width] += jnp.where(wide_row < REACH_Y, tile, 0.0)
        extra = jnp.sum(
            jnp.where(wide_row[:, :128] == 7, extra[:, :128], 0.0), keepdims=True
        )
        set_width = max(128, 2 * knots)
        grid_row = lax.broadcasted_iota(jnp.int32, (grid_rows, set_width), 0)
        grid_lane = lax.broadcasted_iota(jnp.int32, (grid_rows, set_width), 1)
        keep = (
            (grid_row >= 1) & (grid_row <= count_y * cells_y) & (grid_lane < 2 * knots)
        )
        out = []
        for number in range(set_count):
            start = number * 2 * knots
            at = start - start % 128
            part = grid_sum[:, at : at + set_width]
            if start % 128:
                part = pltpu.roll(part, set_width - start % 128, 1)
            out.append(jnp.where(keep, part, 0.0))
        return out, extra

    def window_of(grid):
        picked = jnp.zeros((8, grid.shape[1]), F32)
        for t in range(count_y):
            picked = jnp.where(ty == t, grid[2 * t : 2 * t + 8], picked)
        out = []
        for member in range(2):
            start = member * knots
            at = start - start % 128
            shift = lax.rem(128 + 128 - start % 128 - first_knot, 128)
            part = pltpu.roll(picked[:, at : at + 128], shift, 1)
            out.append(jnp.where(valid, part, 0.0))
        return out

    def dot(left, right):
        return jnp.sum(left * right, keepdims=True)

    def pulled(terms_ref, motion):
        return (
            terms_ref[2] * motion[0] + terms_ref[3] * motion[1],
            terms_ref[3] * motion[0] + terms_ref[4] * motion[1],
        )

    def weighted(weight_ref, pair):
        return [weight_ref[...] * pair[0], weight_ref[...] * pair[1]]

    def density_row(weight_ref, motion, pull):
        dense = weight_ref[...] * (motion[0] * pull[0] + motion[1] * pull[1])
        line = jnp.sum(dense, axis=0, keepdims=True)
        total = line[:, :128]
        for tile in range(1, tiles):
            total = total + line[:, tile * 128 : (tile + 1) * 128]
        return jnp.where(small_row == 7, total, 0.0)

    part = gather_up(
        weighted(coarse_weight, (coarse_terms[0], coarse_terms[1])), coarse_rows, coarse_cols
    )
    send(0, message([part], widths[0]))
    terms_into(fine_image(0), fine_image(1), 1, 1, fixed_minds, moving_minds, fine_terms, breadth)
    fine_start = gather_up(
        weighted(fine_weight, (fine_terms[0], fine_terms[1])), fine_rows, fine_cols
    )
    arrive(0)
    (direction0,), _ = collect(0, 1)
    norm0 = dot(direction0, direction0)

    window = window_of(direction0)
    motion = displace(window, coarse_rows, coarse_cols)
    part = gather_up(
        weighted(coarse_weight, pulled(coarse_terms, motion)), coarse_rows, coarse_cols
    )
    send(1, message([part, fine_start], widths[1]))
    fine_motion0 = displace(window, fine_rows, fine_cols)
    fine_part0 = gather_up(
        weighted(fine_weight, pulled(fine_terms, fine_motion0)), fine_rows, fine_cols
    )
    arrive(1)
    (image0, fine_gradient), _ = collect(1, 2)
    step0 = norm0 / dot(direction0, image0)
    direction1 = direction0 - step0 * image0
    norm1 = dot(direction1, direction1)

    window = window_of(direction1)
    motion = displace(window, coarse_rows, coarse_cols)
    dense = density_row(coarse_weight, motion, pulled(coarse_terms, motion))
    fine_motion1 = displace(window, fine_rows, fine_cols)
    fine_part1 = gather_up(
        weighted(fine_weight, pulled(fine_terms, fine_motion1)), fine_rows, fine_cols
    )
    pieces = message([fine_part0, fine_part1], widths[2])
    pieces[0] = pieces[0] + dense
    send(2, pieces)
    arrive(2)
    (image0, image1), curvature = collect(2, 2)
    step1 = norm1 / curvature
    control = -step0 * direction0 - step1 * direction1
    direction2 = fine_gradient - step0 * image0 - step1 * image1
    norm2 = dot(direction2, direction2)

    window = window_of(direction2)
    motion2 = displace(window, fine_rows, fine_cols)
    part = gather_up(
        weighted(fine_weight, pulled(fine_terms, motion2)), fine_rows, fine_cols
    )
    send(3, message([part], widths[3]))
    field_y = -step0 * fine_motion0[0] - step1 * fine_motion1[0]
    field_x = -step0 * fine_motion0[1] - step1 * fine_motion1[1]
    arrive(3)
    (image2,), _ = collect(3, 1)
    step2 = norm2 / dot(direction2, image2)
    direction3 = direction2 - step2 * image2
    norm3 = dot(direction3, direction3)

    motion3 = displace(window_of(direction3), fine_rows, fine_cols)
    pull3 = pulled(fine_terms, motion3)
    send(4, [density_row(fine_weight, motion3, pull3)])
    control = control - step2 * direction2
    control_window = window_of(control)
    direction_window = window_of(direction3)
    field_y = field_y - step2 * motion2[0]
    field_x = field_x - step2 * motion2[1]
    pull_y, pull_x = pulled(fine_terms, (field_y, field_x))
    constant = (
        fine_terms[5]
        + 2.0 * (fine_terms[0] * field_y + fine_terms[1] * field_x)
        + field_y * pull_y
        + field_x * pull_x
    )
    linear = 2.0 * (
        (fine_terms[0] + pull_y) * motion3[0] + (fine_terms[1] + pull_x) * motion3[1]
    )
    square = motion3[0] * pull3[0] + motion3[1] * pull3[1]
    arrive(4)
    _, curvature = collect(4, 0)
    step3 = norm3 / curvature
    mismatch_ref[...] = constant - step3 * (linear - step3 * square)
    for member in range(2):
        own = control_window[member] - step3 * direction_window[member]
        coef_ref[member] = own[1 : 1 + cells_y, 1 : 1 + cells_x]

    for index, (travel_y, travel_x) in enumerate(travels):

        @pl.when(exists(travel_y, travel_x))
        def _():
            place = landing(travel_y, travel_x)
            pltpu.make_async_copy(place, place, rim_send.at[index]).wait()

    for turn in range(rounds):
        part = boxes[turn].at[0 : count - 1]
        pltpu.make_async_copy(part, part, send_sem.at[turn]).wait()


def shards(count_y, count_x, fixed_image, moving_image, tissue):
    height, breadth = fixed_image.shape
    cells_y, cells_x = height // SPACE, breadth // SPACE
    knots = count_x * cells_x
    count = count_y * count_x
    widths = tuple(-(-sets * 2 * knots // 128) * 128 for sets in (1, 2, 2, 1)) + (128,)
    grid_rows = -(-(cells_y * (count_y - 1) + 8) // 8) * 8
    tall, full_lanes = height + 2 * RIM, breadth + 128
    vmem = pltpu.VMEM
    scratch = [
        vmem((2, tall, breadth), F32),
        vmem((2, tall, 128), F32),
        vmem((2, tall, 128), F32),
        vmem((2 * (breadth // 128 + 1), tall, 128), F32),
        vmem((12, height + 16, full_lanes), F32),
        vmem((12, height + 16, full_lanes), F32),
        vmem((6, height, breadth), F32),
        vmem((6, height // 2, breadth), F32),
        vmem((height, breadth), F32),
        vmem((height // 2, breadth), F32),
        vmem((REACH_Y, height, 128), F32),
        vmem((REACH_Y, height // 2, 128), F32),
        vmem((REACH_X, 8, breadth), F32),
        vmem((REACH_X, 8, breadth), F32),
        vmem((grid_rows, max(max(widths), 128)), F32),
    ]
    scratch += [vmem((count, 8, width), F32) for width in widths]
    scratch += [
        pltpu.SemaphoreType.DMA((8,)),
        pltpu.SemaphoreType.DMA((8,)),
        pltpu.SemaphoreType.DMA((len(widths),)),
        pltpu.SemaphoreType.DMA((len(widths),)),
    ]
    return pl.pallas_call(
        functools.partial(kernel, count_y, count_x, widths),
        out_shape=(
            jax.ShapeDtypeStruct((2, cells_y, cells_x), F32),
            jax.ShapeDtypeStruct((height, breadth), F32),
        ),
        in_specs=[
            pl.BlockSpec(memory_space=pltpu.SMEM),
            pl.BlockSpec(memory_space=pltpu.VMEM),
            pl.BlockSpec(memory_space=pltpu.VMEM),
        ],
        out_specs=(
            pl.BlockSpec(memory_space=pltpu.VMEM),
            pl.BlockSpec(memory_space=pltpu.VMEM),
        ),
        scratch_shapes=scratch,
        compiler_params=pltpu.CompilerParams(
            collective_id=0, has_side_effects=True, vmem_limit_bytes=52 * 1024 * 1024
        ),
    )(tissue, fixed_image, moving_image)


def solution(mesh):
    placed = (P("ty", "tx"), P("ty", "tx"), P("ty", "tx"))
    return jax.shard_map(
        functools.partial(shards, mesh.shape["ty"], mesh.shape["tx"]),
        mesh=mesh,
        in_specs=placed,
        out_specs=(P(None, "ty", "tx"), P("ty", "tx")),
        check_vma=False,
    )
```

```python
import functools

import jax
import jax.numpy as jnp
from jax import lax
from jax.experimental import pallas as pl
from jax.experimental.pallas import tpu as pltpu
from jax.sharding import PartitionSpec as P

SPACE = 32
REACH_Y = 5
REACH_X = 11
RIM = 16
SEGMENT = 16
SET = 32
OWN_SLOT = 7
MESH = pl.DeviceIdType.MESH
F32 = jnp.float32

half_offsets = ((0, 2), (2, 0), (2, 2), (2, -2), (0, 4), (4, 0))
travels = ((-1, 0), (1, 0), (0, -1), (0, 1), (-1, -1), (-1, 1), (1, -1), (1, 1))


def bspline(values):
    magnitude = jnp.abs(values)
    near_part = 2.0 / 3.0 - magnitude * magnitude + 0.5 * magnitude * magnitude * magnitude
    rest = 2.0 - magnitude
    far_part = rest * rest * rest / 6.0
    return jnp.where(magnitude < 1.0, near_part, jnp.where(magnitude < 2.0, far_part, 0.0))


def moved(values, by_y, by_x):
    rows, lanes = values.shape
    if by_x:
        values = pltpu.roll(values, (-by_x) % lanes, 1)
    if by_y:
        values = pltpu.roll(values, (-by_y) % rows, 0)
    return values


def minds_into(image, lane_step, out_ref):
    total = None
    for index, (offset_y, offset_x) in enumerate(half_offsets):
        gap = image - moved(image, offset_y, lane_step * offset_x)
        square = gap * gap
        rows = square + moved(square, 1, 0) + moved(square, -1, 0)
        box = rows + moved(rows, 0, lane_step) + moved(rows, 0, -lane_step)
        other = moved(box, -offset_y, -lane_step * offset_x)
        out_ref[2 * index, : image.shape[0]] = box
        out_ref[2 * index + 1, : image.shape[0]] = other
        both = box + other
        total = both if total is None else total + both
    return -1.0 / (total / 12.0 + 0.9)


def terms_into(fixed, moving, lane_step, factor, fixed_ref, moving_ref, terms_ref, wide):
    rows = fixed.shape[0]
    height = rows - 16
    fixed_scale = minds_into(fixed, lane_step, fixed_ref)[8 : 8 + height, :wide]
    moving_scale = minds_into(moving, lane_step, moving_ref)
    sums = None
    for index in range(12):
        fixed_mind = jnp.exp(fixed_ref[index, 8 : 8 + height, :wide] * fixed_scale)
        mind = jnp.exp(moving_ref[index, :rows] * moving_scale)
        differ = mind[8 : 8 + height, :wide] - fixed_mind
        slope_y = moved(mind[:, :wide], 1, 0) - moved(mind[:, :wide], -1, 0)
        slope_y = slope_y[8 : 8 + height]
        own = mind[8 : 8 + height]
        slope_x = (moved(own, 0, lane_step) - moved(own, 0, -lane_step))[:, :wide]
        parts = (
            differ * slope_y,
            differ * slope_x,
            slope_y * slope_y,
            slope_y * slope_x,
            slope_x * slope_x,
            differ * differ,
        )
        sums = parts if sums is None else tuple(a + b for a, b in zip(sums, parts))
    once = 1.0 / (2.0 * factor)
    scales = (once, once, once * once, once * once, once * once, 1.0)
    for index in range(6):
        terms_ref[index] = sums[index] * scales[index]


def kernel(
    count_y,
    count_x,
    tissue_hbm,
    fixed_hbm,
    moving_hbm,
    coef_ref,
    mismatch_ref,
    mid,
    left_side,
    right_side,
    full,
    fixed_minds,
    moving_minds,
    fine_terms,
    coarse_terms,
    fine_weight,
    coarse_weight,
    fine_rows,
    coarse_rows,
    fine_cols,
    coarse_cols,
    tissue_ref,
    tiles_box,
    scalar_box,
    load_sem,
    rim_send,
    rim_recv,
    tile_send,
    tile_recv,
    scalar_send,
    scalar_recv,
):
    ty = lax.axis_index("ty")
    tx = lax.axis_index("tx")
    count = count_y * count_x
    me = ty * count_x + tx
    height, breadth = fixed_hbm.shape
    knots = count_x * (breadth // SPACE)
    cells_y, cells_x = height // SPACE, breadth // SPACE

    def peer(step):
        other = lax.rem(me + step, count)
        return (other // count_x, lax.rem(other, count_x))

    def for_peers(act):
        if count <= 64:
            for step in range(1, count):
                act(peer(step))
        else:

            def body(step, carry):
                act(peer(step))
                return carry

            lax.fori_loop(1, count, body, 0)

    tissue_load = pltpu.make_async_copy(tissue_hbm, tissue_ref, load_sem.at[2])
    tissue_load.start()
    loads = []
    for image, ref in enumerate((fixed_hbm, moving_hbm)):
        loads.append(
            pltpu.make_async_copy(ref, mid.at[image, RIM : RIM + height], load_sem.at[image])
        )
        loads[image].start()

    low, high = slice(0, RIM), slice(RIM + height, 2 * RIM + height)

    @pl.when(ty == 0)
    def _():
        for ref in (mid, left_side, right_side):
            ref[:, low] = jnp.zeros((2, RIM, ref.shape[2]), F32)

    @pl.when(ty == count_y - 1)
    def _():
        for ref in (mid, left_side, right_side):
            ref[:, high] = jnp.zeros((2, RIM, ref.shape[2]), F32)

    @pl.when(tx == 0)
    def _():
        left_side[...] = jnp.zeros(left_side.shape, F32)

    @pl.when(tx == count_x - 1)
    def _():
        right_side[...] = jnp.zeros(right_side.shape, F32)

    tiles_box[...] = jnp.zeros(tiles_box.shape, F32)

    barrier = pltpu.get_barrier_semaphore()
    for_peers(
        lambda device: pl.semaphore_signal(barrier, 1, device_id=device, device_id_type=MESH)
    )

    lane = lax.broadcasted_iota(jnp.int32, (8, breadth), 1)
    for k in range(REACH_X):
        fine_cols[k] = bspline(lane.astype(F32) / SPACE - (k - 1.0))
        coarse_cols[k] = bspline((lane.astype(F32) + 0.5) / SPACE - (k - 1.0))
    row = lax.broadcasted_iota(jnp.int32, (height, 128), 0).astype(F32)
    coarse_row = lax.broadcasted_iota(jnp.int32, (height // 2, 128), 0).astype(F32)
    for r in range(REACH_Y):
        fine_rows[r] = bspline(row / SPACE - (r - 1.0))
        coarse_rows[r] = bspline((2.0 * coarse_row + 0.5) / SPACE - (r - 1.0))
    even = lax.rem(lane, 2) == 0
    tissue_load.wait()
    for i in range(cells_y):
        line = jnp.zeros((8, breadth), F32)
        for j in range(cells_x):
            value = tissue_ref[i, j].astype(F32)
            inside = (lane >= j * SPACE) & (lane < (j + 1) * SPACE)
            line = jnp.where(inside, value, line)
        half = jnp.where(even, line, 0.0)
        for part in range(SPACE // 8):
            start = i * SPACE + part * 8
            fine_weight[start : start + 8] = line
        for part in range(SPACE // 16):
            start = i * (SPACE // 2) + part * 8
            coarse_weight[start : start + 8] = half

    pl.semaphore_wait(barrier, count - 1)

    def rows_of(travel):
        if travel == 0:
            return slice(0, height), slice(RIM, RIM + height)
        if travel > 0:
            return slice(height - RIM, height), low
        return slice(0, RIM), high

    def landing(travel_y, travel_x):
        ref = mid if travel_x == 0 else (left_side if travel_x > 0 else right_side)
        return ref.at[:, rows_of(travel_y)[1]]

    def exists(travel_y, travel_x):
        to_y, to_x = ty + travel_y, tx + travel_x
        return (to_y >= 0) & (to_y < count_y) & (to_x >= 0) & (to_x < count_x)

    for index, (travel_y, travel_x) in enumerate(travels):

        @pl.when(exists(travel_y, travel_x))
        def _():
            source_rows = rows_of(travel_y)[0]
            if travel_x == 0:
                lanes = slice(0, breadth)
            elif travel_x > 0:
                lanes = slice(breadth - 128, breadth)
            else:
                lanes = slice(0, 128)
            for image, ref in enumerate((fixed_hbm, moving_hbm)):
                pltpu.make_async_remote_copy(
                    src_ref=ref.at[source_rows, lanes],
                    dst_ref=landing(travel_y, travel_x).at[image],
                    send_sem=rim_send.at[index],
                    recv_sem=rim_recv.at[index],
                    device_id=(ty + travel_y, tx + travel_x),
                    device_id_type=MESH,
                ).start()

    for load in loads:
        load.wait()

    for index, (travel_y, travel_x) in enumerate(travels):

        @pl.when(exists(-travel_y, -travel_x))
        def _():
            place = landing(travel_y, travel_x)
            pltpu.make_async_copy(place, place, rim_recv.at[index]).wait()

    tiles = breadth // 128
    side_lane = lax.broadcasted_iota(jnp.int32, (height + 2 * RIM, 128), 1)
    for image in range(2):
        for tile in range(tiles):
            full[image * (tiles + 1) + tile] = mid[image, :, tile * 128 : (tile + 1) * 128]
        full[image * (tiles + 1) + tiles] = jnp.where(
            side_lane < 64, right_side[image], left_side[image]
        )

    def fine_image(image):
        base = image * (tiles + 1)
        return jnp.concatenate(
            [full[base + tile, 8 : height + 24] for tile in range(tiles + 1)], axis=1
        )

    def coarse_image(image):
        base = image * (tiles + 1)
        span = height // 2 + RIM
        summed = jnp.concatenate(
            [
                full[base + tile, pl.ds(0, span, stride=2), :]
                + full[base + tile, pl.ds(1, span, stride=2), :]
                for tile in range(tiles + 1)
            ],
            axis=1,
        )
        return 0.25 * (summed + moved(summed, 0, 1))

    terms_into(
        coarse_image(0), coarse_image(1), 2, 2, fixed_minds, moving_minds, coarse_terms, breadth
    )

    small_lane = lax.broadcasted_iota(jnp.int32, (8, 128), 1)
    small_row = lax.broadcasted_iota(jnp.int32, (8, 128), 0)
    knot = lax.rem(small_lane, SEGMENT)
    knot_x = tx * cells_x - 1 + knot
    knot_y = ty * cells_y - 1 + small_row
    valid = (knot < REACH_X) & (small_row < REACH_Y) & (knot_x >= 0) & (knot_x < knots)
    valid = valid & (knot_y >= 0) & (knot_y < count_y * cells_y)
    own = (small_lane < SET) & (knot >= 1) & (knot <= cells_x)
    own = own & (small_row >= 1) & (small_row <= cells_y)

    def displace(window, rows_ref, cols_ref, number=0):
        fields = []
        for member in range(2):
            line = None
            for k in range(REACH_X):
                at = number * SET + member * SEGMENT + k
                part = window[:, at : at + 1] * cols_ref[k]
                line = part if line is None else line + part
            field = None
            for r in range(REACH_Y):
                weights = jnp.concatenate([rows_ref[r]] * tiles, axis=1)
                part = weights * line[r : r + 1, :]
                field = part if field is None else field + part
            fields.append(field)
        return fields

    def gather_up(pixels, rows_ref, cols_ref, number=0):
        out = jnp.zeros((8, 128), F32)
        for member in range(2):
            lines = []
            for r in range(REACH_Y):
                weights = jnp.concatenate([rows_ref[r]] * tiles, axis=1)
                lines.append(jnp.sum(weights * pixels[member], axis=0, keepdims=True))
            lines.append(jnp.zeros((8 - REACH_Y, breadth), F32))
            line = jnp.concatenate(lines, axis=0)
            for k in range(REACH_X):
                column = jnp.sum(line * cols_ref[k], axis=1, keepdims=True)
                at = number * SET + member * SEGMENT + k
                out = jnp.where(small_lane == at, column, out)
        return out

    def slot_of(by_y, by_x):
        return (by_y + 2) * 3 + by_x + 1

    around = [(y, x) for y in range(-2, 3) for x in range(-1, 2) if (y, x) != (0, 0)]

    def send_tile(turn, tile):
        tiles_box[turn, OWN_SLOT] = tile
        for by_y, by_x in around:

            @pl.when(exists(by_y, by_x))
            def _():
                slot = slot_of(-by_y, -by_x)
                pltpu.make_async_remote_copy(
                    src_ref=tiles_box.at[turn, OWN_SLOT],
                    dst_ref=tiles_box.at[turn, slot],
                    send_sem=tile_send.at[slot],
                    recv_sem=tile_recv.at[turn, slot],
                    device_id=(ty + by_y, tx + by_x),
                    device_id_type=MESH,
                ).start()

    def collect_tiles(turn):
        for by_y, by_x in around:

            @pl.when(exists(by_y, by_x))
            def _():
                slot = slot_of(by_y, by_x)
                place = tiles_box.at[turn, slot]
                pltpu.make_async_copy(place, place, tile_recv.at[turn, slot]).wait()

        window = None
        for by_x in range(-1, 2):
            total = None
            for by_y in range(-2, 3):
                part = tiles_box[turn, slot_of(by_y, by_x)]
                if by_y:
                    part = pltpu.roll(part, (2 * by_y) % 8, 0)
                if by_y == 2:
                    part = jnp.where(small_row >= 4, part, 0.0)
                if by_y == -2:
                    part = jnp.where(small_row < 1, part, 0.0)
                total = part if total is None else total + part
            if by_x:
                total = pltpu.roll(total, (8 * by_x) % 128, 1)
                reached = (knot >= 8) if by_x > 0 else (knot < REACH_X - 8)
                total = jnp.where(reached, total, 0.0)
            window = total if window is None else window + total
        return jnp.where(valid, window, 0.0)

    def send_scalars(turn, row):
        scalar_box[turn, me] = row

        def act(device):
            pltpu.make_async_remote_copy(
                src_ref=scalar_box.at[turn, me],
                dst_ref=scalar_box.at[turn, me],
                send_sem=scalar_send.at[turn],
                recv_sem=scalar_recv.at[turn],
                device_id=device,
                device_id_type=MESH,
            ).start()

        for_peers(act)

    def collect_scalars(turn):
        part = scalar_box.at[turn, 0 : count - 1]
        pltpu.make_async_copy(part, part, scalar_recv.at[turn]).wait()
        row = jnp.sum(scalar_box[turn], axis=0)
        lanes = lax.broadcasted_iota(jnp.int32, (1, 128), 1)
        return [
            jnp.sum(
                jnp.where((lanes >= SET * i) & (lanes < SET * (i + 1)), row, 0.0), keepdims=True
            )
            for i in range(4)
        ]

    def scalars(first, second, dense):
        third = jnp.where(own, second * second, 0.0)
        middle = jnp.where(own, first * second, 0.0)
        lead = jnp.where(own, first * first, 0.0)
        packed = lead + pltpu.roll(middle, SET, 1) + pltpu.roll(third, 2 * SET, 1)
        row = jnp.sum(packed, axis=0, keepdims=True)
        dense = dense + pltpu.roll(dense, 64, 1)
        dense = dense + pltpu.roll(dense, 32, 1)
        lanes = lax.broadcasted_iota(jnp.int32, (1, 128), 1)
        return jnp.where(lanes >= 3 * SET, dense, row)

    def pulled(terms_ref, motion):
        return (
            terms_ref[2] * motion[0] + terms_ref[3] * motion[1],
            terms_ref[3] * motion[0] + terms_ref[4] * motion[1],
        )

    def weighted(weight_ref, pair):
        return [weight_ref[...] * pair[0], weight_ref[...] * pair[1]]

    def density_row(weight_ref, motion, pull):
        dense = weight_ref[...] * (motion[0] * pull[0] + motion[1] * pull[1])
        line = jnp.sum(dense, axis=0, keepdims=True)
        total = line[:, :128]
        for tile in range(1, tiles):
            total = total + line[:, tile * 128 : (tile + 1) * 128]
        return total

    def steps_of(first, middle, third, fourth):
        step = first / middle
        norm = first - 2.0 * step * middle + step * step * third
        curvature = middle - 2.0 * step * third + step * step * fourth
        return step, norm / curvature

    send_tile(
        0,
        gather_up(
            weighted(coarse_weight, (coarse_terms[0], coarse_terms[1])), coarse_rows, coarse_cols
        ),
    )
    terms_into(fine_image(0), fine_image(1), 1, 1, fixed_minds, moving_minds, fine_terms, breadth)
    fine_start = gather_up(
        weighted(fine_weight, (fine_terms[0], fine_terms[1])), fine_rows, fine_cols, 1
    )
    gradient0 = collect_tiles(0)

    motion = displace(gradient0, coarse_rows, coarse_cols)
    part = gather_up(
        weighted(coarse_weight, pulled(coarse_terms, motion)), coarse_rows, coarse_cols
    )
    send_tile(1, part + fine_start)
    fine_motion0 = displace(gradient0, fine_rows, fine_cols)
    fine_part0 = gather_up(
        weighted(fine_weight, pulled(fine_terms, fine_motion0)), fine_rows, fine_cols
    )
    gradient1 = collect_tiles(1)

    motion = displace(gradient1, coarse_rows, coarse_cols)
    dense = density_row(coarse_weight, motion, pulled(coarse_terms, motion))
    send_scalars(0, scalars(gradient0, gradient1, dense))
    fine_motion1 = displace(gradient1, fine_rows, fine_cols)
    fine_part1 = gather_up(
        weighted(fine_weight, pulled(fine_terms, fine_motion1)), fine_rows, fine_cols, 1
    )
    send_tile(2, fine_part0 + fine_part1)
    fine_gradient = pltpu.roll(gradient1, 128 - SET, 1)
    images = collect_tiles(2)
    step0, step1 = steps_of(*collect_scalars(0))
    near, far = -(step0 + step1), step0 * step1
    control = near * gradient0 + far * gradient1
    direction = fine_gradient + near * images + far * pltpu.roll(images, 128 - SET, 1)

    motion2 = displace(direction, fine_rows, fine_cols)
    send_tile(
        3,
        gather_up(weighted(fine_weight, pulled(fine_terms, motion2)), fine_rows, fine_cols),
    )
    field_y = near * fine_motion0[0] + far * fine_motion1[0]
    field_x = near * fine_motion0[1] + far * fine_motion1[1]
    image = collect_tiles(3)

    motion3 = displace(image, fine_rows, fine_cols)
    dense = density_row(fine_weight, motion3, pulled(fine_terms, motion3))
    send_scalars(1, scalars(direction, image, dense))
    step0, step1 = steps_of(*collect_scalars(1))
    near, far = -(step0 + step1), step0 * step1
    control = control + near * direction + far * image
    field_y = field_y + near * motion2[0] + far * motion3[0]
    field_x = field_x + near * motion2[1] + far * motion3[1]
    pull_y, pull_x = pulled(fine_terms, (field_y, field_x))
    mismatch_ref[...] = (
        fine_terms[5]
        + 2.0 * (fine_terms[0] * field_y + fine_terms[1] * field_x)
        + field_y * pull_y
        + field_x * pull_x
    )
    for member in range(2):
        start = member * SEGMENT + 1
        coef_ref[member] = control[1 : 1 + cells_y, start : start + cells_x]

    for index, (travel_y, travel_x) in enumerate(travels):

        @pl.when(exists(travel_y, travel_x))
        def _():
            place = landing(travel_y, travel_x)
            pltpu.make_async_copy(place, place, rim_send.at[index]).wait()

    for by_y, by_x in around:

        @pl.when(exists(by_y, by_x))
        def _():
            slot = slot_of(-by_y, -by_x)
            place = tiles_box.at[:, slot]
            pltpu.make_async_copy(place, place, tile_send.at[slot]).wait()

    for turn in range(2):
        part = scalar_box.at[turn, 0 : count - 1]
        pltpu.make_async_copy(part, part, scalar_send.at[turn]).wait()


def shards(count_y, count_x, fixed_image, moving_image, tissue):
    height, breadth = fixed_image.shape
    cells_y, cells_x = height // SPACE, breadth // SPACE
    count = count_y * count_x
    tall, full_lanes = height + 2 * RIM, breadth + 128
    vmem = pltpu.VMEM
    scratch = [
        vmem((2, tall, breadth), F32),
        vmem((2, tall, 128), F32),
        vmem((2, tall, 128), F32),
        vmem((2 * (breadth // 128 + 1), tall, 128), F32),
        vmem((12, height + 16, full_lanes), F32),
        vmem((12, height + 16, full_lanes), F32),
        vmem((6, height, breadth), F32),
        vmem((6, height // 2, breadth), F32),
        vmem((height, breadth), F32),
        vmem((height // 2, breadth), F32),
        vmem((REACH_Y, height, 128), F32),
        vmem((REACH_Y, height // 2, 128), F32),
        vmem((REACH_X, 8, breadth), F32),
        vmem((REACH_X, 8, breadth), F32),
        pltpu.SMEM((cells_y, cells_x), jnp.int32),
        vmem((4, 15, 8, 128), F32),
        vmem((2, count, 1, 128), F32),
        pltpu.SemaphoreType.DMA((3,)),
        pltpu.SemaphoreType.DMA((8,)),
        pltpu.SemaphoreType.DMA((8,)),
        pltpu.SemaphoreType.DMA((15,)),
        pltpu.SemaphoreType.DMA((4, 15)),
        pltpu.SemaphoreType.DMA((2,)),
        pltpu.SemaphoreType.DMA((2,)),
    ]
    return pl.pallas_call(
        functools.partial(kernel, count_y, count_x),
        out_shape=(
            jax.ShapeDtypeStruct((2, cells_y, cells_x), F32),
            jax.ShapeDtypeStruct((height, breadth), F32),
        ),
        in_specs=[
            pl.BlockSpec(memory_space=pltpu.HBM),
            pl.BlockSpec(memory_space=pltpu.HBM),
            pl.BlockSpec(memory_space=pltpu.HBM),
        ],
        out_specs=(
            pl.BlockSpec(memory_space=pltpu.VMEM),
            pl.BlockSpec(memory_space=pltpu.VMEM),
        ),
        scratch_shapes=scratch,
        compiler_params=pltpu.CompilerParams(
            collective_id=0, has_side_effects=True, vmem_limit_bytes=52 * 1024 * 1024
        ),
    )(tissue, fixed_image, moving_image)


def solution(mesh):
    placed = (P("ty", "tx"), P("ty", "tx"), P("ty", "tx"))
    return jax.shard_map(
        functools.partial(shards, mesh.shape["ty"], mesh.shape["tx"]),
        mesh=mesh,
        in_specs=placed,
        out_specs=(P(None, "ty", "tx"), P("ty", "tx")),
        check_vma=False,
    )
```

```python
import functools

import jax
import jax.numpy as jnp
from jax import lax
from jax.experimental import pallas as pl
from jax.experimental.pallas import tpu as pltpu
from jax.sharding import PartitionSpec as P

SPACE = 32
REACH_Y = 5
REACH_X = 11
RIM = 16
SEGMENT = 16
SET = 32
OWN_SLOT = 7
MESH = pl.DeviceIdType.MESH
F32 = jnp.float32

half_offsets = ((0, 2), (2, 0), (2, 2), (2, -2), (0, 4), (4, 0))
travels = ((-1, 0), (1, 0), (0, -1), (0, 1), (-1, -1), (-1, 1), (1, -1), (1, 1))


def bspline(values):
    magnitude = jnp.abs(values)
    near_part = 2.0 / 3.0 - magnitude * magnitude + 0.5 * magnitude * magnitude * magnitude
    rest = 2.0 - magnitude
    far_part = rest * rest * rest / 6.0
    return jnp.where(magnitude < 1.0, near_part, jnp.where(magnitude < 2.0, far_part, 0.0))


def moved(values, by_y, by_x):
    rows, lanes = values.shape
    if by_x:
        values = pltpu.roll(values, (-by_x) % lanes, 1)
    if by_y:
        values = pltpu.roll(values, (-by_y) % rows, 0)
    return values


def minds_into(image, lane_step, out_ref):
    total = None
    for index, (offset_y, offset_x) in enumerate(half_offsets):
        gap = image - moved(image, offset_y, lane_step * offset_x)
        square = gap * gap
        rows = square + moved(square, 1, 0) + moved(square, -1, 0)
        box = rows + moved(rows, 0, lane_step) + moved(rows, 0, -lane_step)
        other = moved(box, -offset_y, -lane_step * offset_x)
        out_ref[2 * index, : image.shape[0]] = box
        out_ref[2 * index + 1, : image.shape[0]] = other
        both = box + other
        total = both if total is None else total + both
    return -1.0 / (total / 12.0 + 0.9)


def terms_into(fixed, moving, lane_step, factor, fixed_ref, moving_ref, terms_ref, wide):
    rows = fixed.shape[0]
    height = rows - 16
    fixed_scale = minds_into(fixed, lane_step, fixed_ref)[8 : 8 + height, :wide]
    moving_scale = minds_into(moving, lane_step, moving_ref)
    sums = None
    for index in range(12):
        fixed_mind = jnp.exp(fixed_ref[index, 8 : 8 + height, :wide] * fixed_scale)
        mind = jnp.exp(moving_ref[index, :rows] * moving_scale)
        differ = mind[8 : 8 + height, :wide] - fixed_mind
        slope_y = moved(mind[:, :wide], 1, 0) - moved(mind[:, :wide], -1, 0)
        slope_y = slope_y[8 : 8 + height]
        own = mind[8 : 8 + height]
        slope_x = (moved(own, 0, lane_step) - moved(own, 0, -lane_step))[:, :wide]
        parts = (
            differ * slope_y,
            differ * slope_x,
            slope_y * slope_y,
            slope_y * slope_x,
            slope_x * slope_x,
            differ * differ,
        )
        sums = parts if sums is None else tuple(a + b for a, b in zip(sums, parts))
    once = 1.0 / (2.0 * factor)
    scales = (once, once, once * once, once * once, once * once, 1.0)
    for index in range(6):
        terms_ref[index] = sums[index] * scales[index]


def kernel(
    count_y,
    count_x,
    tissue_hbm,
    fixed_hbm,
    moving_hbm,
    coef_ref,
    mismatch_ref,
    mid,
    left_side,
    right_side,
    full,
    fixed_minds,
    moving_minds,
    fine_terms,
    coarse_terms,
    fine_weight,
    coarse_weight,
    fine_rows,
    coarse_rows,
    fine_cols,
    coarse_cols,
    tissue_ref,
    tiles_box,
    scalar_box,
    load_sem,
    rim_send,
    rim_recv,
    tile_send,
    tile_recv,
    scalar_send,
    scalar_recv,
):
    ty = lax.axis_index("ty")
    tx = lax.axis_index("tx")
    count = count_y * count_x
    me = ty * count_x + tx
    height, breadth = fixed_hbm.shape
    knots = count_x * (breadth // SPACE)
    cells_y, cells_x = height // SPACE, breadth // SPACE

    def peer(step):
        other = lax.rem(me + step, count)
        return (other // count_x, lax.rem(other, count_x))

    def for_peers(act):
        if count <= 64:
            for step in range(1, count):
                act(peer(step))
        else:

            def body(step, carry):
                act(peer(step))
                return carry

            lax.fori_loop(1, count, body, 0)

    tissue_load = pltpu.make_async_copy(tissue_hbm, tissue_ref, load_sem.at[2])
    tissue_load.start()
    loads = []
    for image, ref in enumerate((fixed_hbm, moving_hbm)):
        loads.append(
            pltpu.make_async_copy(ref, mid.at[image, RIM : RIM + height], load_sem.at[image])
        )
        loads[image].start()

    low, high = slice(0, RIM), slice(RIM + height, 2 * RIM + height)

    @pl.when(ty == 0)
    def _():
        for ref in (mid, left_side, right_side):
            ref[:, low] = jnp.zeros((2, RIM, ref.shape[2]), F32)

    @pl.when(ty == count_y - 1)
    def _():
        for ref in (mid, left_side, right_side):
            ref[:, high] = jnp.zeros((2, RIM, ref.shape[2]), F32)

    @pl.when(tx == 0)
    def _():
        left_side[...] = jnp.zeros(left_side.shape, F32)

    @pl.when(tx == count_x - 1)
    def _():
        right_side[...] = jnp.zeros(right_side.shape, F32)

    tiles_box[...] = jnp.zeros(tiles_box.shape, F32)

    barrier = pltpu.get_barrier_semaphore()
    near = 2 <= count_y <= 8 and 2 <= count_x <= 4
    greeted = [(y, x) for y in range(-1, 2) for x in range(-1, 2) if (y, x) != (0, 0)]
    if count_y == 8:
        greeted += [(1 - count_y, 0), (count_y - 1, 0)]

    def here(by_y, by_x):
        to_y, to_x = ty + by_y, tx + by_x
        return (to_y >= 0) & (to_y < count_y) & (to_x >= 0) & (to_x < count_x)

    def greet(device):
        pl.semaphore_signal(barrier, 1, device_id=device, device_id_type=MESH)

    if near:
        for by_y, by_x in greeted:

            @pl.when(here(by_y, by_x))
            def _():
                greet((ty + by_y, tx + by_x))

    else:
        for_peers(greet)

    lane = lax.broadcasted_iota(jnp.int32, (8, breadth), 1)
    for k in range(REACH_X):
        fine_cols[k] = bspline(lane.astype(F32) / SPACE - (k - 1.0))
        coarse_cols[k] = bspline((lane.astype(F32) + 0.5) / SPACE - (k - 1.0))
    row = lax.broadcasted_iota(jnp.int32, (height, 128), 0).astype(F32)
    coarse_row = lax.broadcasted_iota(jnp.int32, (height // 2, 128), 0).astype(F32)
    for r in range(REACH_Y):
        fine_rows[r] = bspline(row / SPACE - (r - 1.0))
        coarse_rows[r] = bspline((2.0 * coarse_row + 0.5) / SPACE - (r - 1.0))
    even = lax.rem(lane, 2) == 0
    tissue_load.wait()
    for i in range(cells_y):
        line = jnp.zeros((8, breadth), F32)
        for j in range(cells_x):
            value = tissue_ref[i, j].astype(F32)
            inside = (lane >= j * SPACE) & (lane < (j + 1) * SPACE)
            line = jnp.where(inside, value, line)
        half = jnp.where(even, line, 0.0)
        for part in range(SPACE // 8):
            start = i * SPACE + part * 8
            fine_weight[start : start + 8] = line
        for part in range(SPACE // 16):
            start = i * (SPACE // 2) + part * 8
            coarse_weight[start : start + 8] = half

    if near:
        edge_y = jnp.where((ty == 0) | (ty == count_y - 1), 1, 0)
        edge_x = jnp.where((tx == 0) | (tx == count_x - 1), 1, 0)
        greeters = (3 - edge_y) * (3 - edge_x) - 1
        if count_y == 8:
            greeters = greeters + edge_y
        pl.semaphore_wait(barrier, greeters)
    else:
        pl.semaphore_wait(barrier, count - 1)

    def rows_of(travel):
        if travel == 0:
            return slice(0, height), slice(RIM, RIM + height)
        if travel > 0:
            return slice(height - RIM, height), low
        return slice(0, RIM), high

    def landing(travel_y, travel_x):
        ref = mid if travel_x == 0 else (left_side if travel_x > 0 else right_side)
        return ref.at[:, rows_of(travel_y)[1]]

    def exists(travel_y, travel_x):
        to_y, to_x = ty + travel_y, tx + travel_x
        return (to_y >= 0) & (to_y < count_y) & (to_x >= 0) & (to_x < count_x)

    for index, (travel_y, travel_x) in enumerate(travels):

        @pl.when(exists(travel_y, travel_x))
        def _():
            source_rows = rows_of(travel_y)[0]
            if travel_x == 0:
                lanes = slice(0, breadth)
            elif travel_x > 0:
                lanes = slice(breadth - 128, breadth)
            else:
                lanes = slice(0, 128)
            for image, ref in enumerate((fixed_hbm, moving_hbm)):
                pltpu.make_async_remote_copy(
                    src_ref=ref.at[source_rows, lanes],
                    dst_ref=landing(travel_y, travel_x).at[image],
                    send_sem=rim_send.at[index],
                    recv_sem=rim_recv.at[index],
                    device_id=(ty + travel_y, tx + travel_x),
                    device_id_type=MESH,
                ).start()

    for load in loads:
        load.wait()

    for index, (travel_y, travel_x) in enumerate(travels):

        @pl.when(exists(-travel_y, -travel_x))
        def _():
            place = landing(travel_y, travel_x)
            pltpu.make_async_copy(place, place, rim_recv.at[index]).wait()

    tiles = breadth // 128
    side_lane = lax.broadcasted_iota(jnp.int32, (height + 2 * RIM, 128), 1)
    for image in range(2):
        for tile in range(tiles):
            full[image * (tiles + 1) + tile] = mid[image, :, tile * 128 : (tile + 1) * 128]
        full[image * (tiles + 1) + tiles] = jnp.where(
            side_lane < 64, right_side[image], left_side[image]
        )

    def fine_image(image):
        base = image * (tiles + 1)
        return jnp.concatenate(
            [full[base + tile, 8 : height + 24] for tile in range(tiles + 1)], axis=1
        )

    def coarse_image(image):
        base = image * (tiles + 1)
        span = height // 2 + RIM
        summed = jnp.concatenate(
            [
                full[base + tile, pl.ds(0, span, stride=2), :]
                + full[base + tile, pl.ds(1, span, stride=2), :]
                for tile in range(tiles + 1)
            ],
            axis=1,
        )
        return 0.25 * (summed + moved(summed, 0, 1))

    terms_into(
        coarse_image(0), coarse_image(1), 2, 2, fixed_minds, moving_minds, coarse_terms, breadth
    )

    small_lane = lax.broadcasted_iota(jnp.int32, (8, 128), 1)
    small_row = lax.broadcasted_iota(jnp.int32, (8, 128), 0)
    knot = lax.rem(small_lane, SEGMENT)
    knot_x = tx * cells_x - 1 + knot
    knot_y = ty * cells_y - 1 + small_row
    valid = (knot < REACH_X) & (small_row < REACH_Y) & (knot_x >= 0) & (knot_x < knots)
    valid = valid & (knot_y >= 0) & (knot_y < count_y * cells_y)
    own = (small_lane < SET) & (knot >= 1) & (knot <= cells_x)
    own = own & (small_row >= 1) & (small_row <= cells_y)

    def displace(window, rows_ref, cols_ref, number=0):
        fields = []
        for member in range(2):
            line = None
            for k in range(REACH_X):
                at = number * SET + member * SEGMENT + k
                part = window[:, at : at + 1] * cols_ref[k]
                line = part if line is None else line + part
            field = None
            for r in range(REACH_Y):
                weights = jnp.concatenate([rows_ref[r]] * tiles, axis=1)
                part = weights * line[r : r + 1, :]
                field = part if field is None else field + part
            fields.append(field)
        return fields

    def gather_up(pixels, rows_ref, cols_ref, number=0):
        out = jnp.zeros((8, 128), F32)
        for member in range(2):
            lines = []
            for r in range(REACH_Y):
                weights = jnp.concatenate([rows_ref[r]] * tiles, axis=1)
                lines.append(jnp.sum(weights * pixels[member], axis=0, keepdims=True))
            lines.append(jnp.zeros((8 - REACH_Y, breadth), F32))
            line = jnp.concatenate(lines, axis=0)
            for k in range(REACH_X):
                column = jnp.sum(line * cols_ref[k], axis=1, keepdims=True)
                at = number * SET + member * SEGMENT + k
                out = jnp.where(small_lane == at, column, out)
        return out

    def slot_of(by_y, by_x):
        return (by_y + 2) * 3 + by_x + 1

    around = [(y, x) for y in range(-2, 3) for x in range(-1, 2) if (y, x) != (0, 0)]

    def send_tile(turn, tile):
        tiles_box[turn, OWN_SLOT] = tile
        for by_y, by_x in around:

            @pl.when(exists(by_y, by_x))
            def _():
                slot = slot_of(-by_y, -by_x)
                pltpu.make_async_remote_copy(
                    src_ref=tiles_box.at[turn, OWN_SLOT],
                    dst_ref=tiles_box.at[turn, slot],
                    send_sem=tile_send.at[slot],
                    recv_sem=tile_recv.at[turn, slot],
                    device_id=(ty + by_y, tx + by_x),
                    device_id_type=MESH,
                ).start()

    def collect_tiles(turn):
        for by_y, by_x in around:

            @pl.when(exists(by_y, by_x))
            def _():
                slot = slot_of(by_y, by_x)
                place = tiles_box.at[turn, slot]
                pltpu.make_async_copy(place, place, tile_recv.at[turn, slot]).wait()

        window = None
        for by_x in range(-1, 2):
            total = None
            for by_y in range(-2, 3):
                part = tiles_box[turn, slot_of(by_y, by_x)]
                if by_y:
                    part = pltpu.roll(part, (2 * by_y) % 8, 0)
                if by_y == 2:
                    part = jnp.where(small_row >= 4, part, 0.0)
                if by_y == -2:
                    part = jnp.where(small_row < 1, part, 0.0)
                total = part if total is None else total + part
            if by_x:
                total = pltpu.roll(total, (8 * by_x) % 128, 1)
                reached = (knot >= 8) if by_x > 0 else (knot < REACH_X - 8)
                total = jnp.where(reached, total, 0.0)
            window = total if window is None else window + total
        return jnp.where(valid, window, 0.0)

    def send_scalars(turn, row):
        scalar_box[turn, me] = row

        def act(device):
            pltpu.make_async_remote_copy(
                src_ref=scalar_box.at[turn, me],
                dst_ref=scalar_box.at[turn, me],
                send_sem=scalar_send.at[turn],
                recv_sem=scalar_recv.at[turn],
                device_id=device,
                device_id_type=MESH,
            ).start()

        for_peers(act)

    def collect_scalars(turn):
        part = scalar_box.at[turn, 0 : count - 1]
        pltpu.make_async_copy(part, part, scalar_recv.at[turn]).wait()
        row = jnp.sum(scalar_box[turn], axis=0)
        lanes = lax.broadcasted_iota(jnp.int32, (1, 128), 1)
        return [
            jnp.sum(
                jnp.where((lanes >= SET * i) & (lanes < SET * (i + 1)), row, 0.0), keepdims=True
            )
            for i in range(4)
        ]

    def scalars(first, second, dense):
        third = jnp.where(own, second * second, 0.0)
        middle = jnp.where(own, first * second, 0.0)
        lead = jnp.where(own, first * first, 0.0)
        packed = lead + pltpu.roll(middle, SET, 1) + pltpu.roll(third, 2 * SET, 1)
        row = jnp.sum(packed, axis=0, keepdims=True)
        dense = dense + pltpu.roll(dense, 64, 1)
        dense = dense + pltpu.roll(dense, 32, 1)
        lanes = lax.broadcasted_iota(jnp.int32, (1, 128), 1)
        return jnp.where(lanes >= 3 * SET, dense, row)

    def pulled(terms_ref, motion):
        return (
            terms_ref[2] * motion[0] + terms_ref[3] * motion[1],
            terms_ref[3] * motion[0] + terms_ref[4] * motion[1],
        )

    def weighted(weight_ref, pair):
        return [weight_ref[...] * pair[0], weight_ref[...] * pair[1]]

    def density_row(weight_ref, motion, pull):
        dense = weight_ref[...] * (motion[0] * pull[0] + motion[1] * pull[1])
        line = jnp.sum(dense, axis=0, keepdims=True)
        total = line[:, :128]
        for tile in range(1, tiles):
            total = total + line[:, tile * 128 : (tile + 1) * 128]
        return total

    def steps_of(first, middle, third, fourth):
        step = first / middle
        norm = first - 2.0 * step * middle + step * step * third
        curvature = middle - 2.0 * step * third + step * step * fourth
        return step, norm / curvature

    send_tile(
        0,
        gather_up(
            weighted(coarse_weight, (coarse_terms[0], coarse_terms[1])), coarse_rows, coarse_cols
        ),
    )
    terms_into(fine_image(0), fine_image(1), 1, 1, fixed_minds, moving_minds, fine_terms, breadth)
    fine_start = gather_up(
        weighted(fine_weight, (fine_terms[0], fine_terms[1])), fine_rows, fine_cols, 1
    )
    gradient0 = collect_tiles(0)

    motion = displace(gradient0, coarse_rows, coarse_cols)
    part = gather_up(
        weighted(coarse_weight, pulled(coarse_terms, motion)), coarse_rows, coarse_cols
    )
    send_tile(1, part + fine_start)
    fine_motion0 = displace(gradient0, fine_rows, fine_cols)
    fine_part0 = gather_up(
        weighted(fine_weight, pulled(fine_terms, fine_motion0)), fine_rows, fine_cols
    )
    gradient1 = collect_tiles(1)

    motion = displace(gradient1, coarse_rows, coarse_cols)
    dense = density_row(coarse_weight, motion, pulled(coarse_terms, motion))
    send_scalars(0, scalars(gradient0, gradient1, dense))
    fine_motion1 = displace(gradient1, fine_rows, fine_cols)
    fine_part1 = gather_up(
        weighted(fine_weight, pulled(fine_terms, fine_motion1)), fine_rows, fine_cols, 1
    )
    send_tile(2, fine_part0 + fine_part1)
    fine_gradient = pltpu.roll(gradient1, 128 - SET, 1)
    images = collect_tiles(2)
    step0, step1 = steps_of(*collect_scalars(0))
    near, far = -(step0 + step1), step0 * step1
    control = near * gradient0 + far * gradient1
    direction = fine_gradient + near * images + far * pltpu.roll(images, 128 - SET, 1)

    motion2 = displace(direction, fine_rows, fine_cols)
    send_tile(
        3,
        gather_up(weighted(fine_weight, pulled(fine_terms, motion2)), fine_rows, fine_cols),
    )
    field_y = near * fine_motion0[0] + far * fine_motion1[0]
    field_x = near * fine_motion0[1] + far * fine_motion1[1]
    image = collect_tiles(3)

    motion3 = displace(image, fine_rows, fine_cols)
    dense = density_row(fine_weight, motion3, pulled(fine_terms, motion3))
    send_scalars(1, scalars(direction, image, dense))
    step0, step1 = steps_of(*collect_scalars(1))
    near, far = -(step0 + step1), step0 * step1
    control = control + near * direction + far * image
    field_y = field_y + near * motion2[0] + far * motion3[0]
    field_x = field_x + near * motion2[1] + far * motion3[1]
    pull_y, pull_x = pulled(fine_terms, (field_y, field_x))
    mismatch_ref[...] = (
        fine_terms[5]
        + 2.0 * (fine_terms[0] * field_y + fine_terms[1] * field_x)
        + field_y * pull_y
        + field_x * pull_x
    )
    for member in range(2):
        start = member * SEGMENT + 1
        coef_ref[member] = control[1 : 1 + cells_y, start : start + cells_x]

    for index, (travel_y, travel_x) in enumerate(travels):

        @pl.when(exists(travel_y, travel_x))
        def _():
            place = landing(travel_y, travel_x)
            pltpu.make_async_copy(place, place, rim_send.at[index]).wait()

    for by_y, by_x in around:

        @pl.when(exists(by_y, by_x))
        def _():
            slot = slot_of(-by_y, -by_x)
            place = tiles_box.at[:, slot]
            pltpu.make_async_copy(place, place, tile_send.at[slot]).wait()

    for turn in range(2):
        part = scalar_box.at[turn, 0 : count - 1]
        pltpu.make_async_copy(part, part, scalar_send.at[turn]).wait()


def shards(count_y, count_x, fixed_image, moving_image, tissue):
    height, breadth = fixed_image.shape
    cells_y, cells_x = height // SPACE, breadth // SPACE
    count = count_y * count_x
    tall, full_lanes = height + 2 * RIM, breadth + 128
    vmem = pltpu.VMEM
    scratch = [
        vmem((2, tall, breadth), F32),
        vmem((2, tall, 128), F32),
        vmem((2, tall, 128), F32),
        vmem((2 * (breadth // 128 + 1), tall, 128), F32),
        vmem((12, height + 16, full_lanes), F32),
        vmem((12, height + 16, full_lanes), F32),
        vmem((6, height, breadth), F32),
        vmem((6, height // 2, breadth), F32),
        vmem((height, breadth), F32),
        vmem((height // 2, breadth), F32),
        vmem((REACH_Y, height, 128), F32),
        vmem((REACH_Y, height // 2, 128), F32),
        vmem((REACH_X, 8, breadth), F32),
        vmem((REACH_X, 8, breadth), F32),
        pltpu.SMEM((cells_y, cells_x), jnp.int32),
        vmem((4, 15, 8, 128), F32),
        vmem((2, count, 1, 128), F32),
        pltpu.SemaphoreType.DMA((3,)),
        pltpu.SemaphoreType.DMA((8,)),
        pltpu.SemaphoreType.DMA((8,)),
        pltpu.SemaphoreType.DMA((15,)),
        pltpu.SemaphoreType.DMA((4, 15)),
        pltpu.SemaphoreType.DMA((2,)),
        pltpu.SemaphoreType.DMA((2,)),
    ]
    return pl.pallas_call(
        functools.partial(kernel, count_y, count_x),
        out_shape=(
            jax.ShapeDtypeStruct((2, cells_y, cells_x), F32),
            jax.ShapeDtypeStruct((height, breadth), F32),
        ),
        in_specs=[
            pl.BlockSpec(memory_space=pltpu.HBM),
            pl.BlockSpec(memory_space=pltpu.HBM),
            pl.BlockSpec(memory_space=pltpu.HBM),
        ],
        out_specs=(
            pl.BlockSpec(memory_space=pltpu.VMEM),
            pl.BlockSpec(memory_space=pltpu.VMEM),
        ),
        scratch_shapes=scratch,
        compiler_params=pltpu.CompilerParams(
            collective_id=0, has_side_effects=True, vmem_limit_bytes=63 * 1024 * 1024
        ),
    )(tissue, fixed_image, moving_image)


def solution(mesh):
    placed = (P("ty", "tx"), P("ty", "tx"), P("ty", "tx"))
    return jax.shard_map(
        functools.partial(shards, mesh.shape["ty"], mesh.shape["tx"]),
        mesh=mesh,
        in_specs=placed,
        out_specs=(P(None, "ty", "tx"), P("ty", "tx")),
        check_vma=False,
    )
```
